32 devices in a mesh: tsink: 4 (over y, x), mom: 8 (over z, core).
Axes of the slice: x: 2, y: 2, z: 4, core: 2. Of those that a mesh axis runs over, the one named last changes fastest.
Arguments:
- perambulators: bfloat16 [4, 4, 1024, 1024], P('tsink'), may hold values from -0.1875 to 0.1875
- elementals: bfloat16 [4, 8, 1024, 1024], P('tsink', 'mom'), may hold values from -6 to 6
- src_times: int32 [4], replicated, may hold values from 0 to 3, as said below
- diagrams: int32 [64, 2], replicated, may hold values from 0 to 7
Outputs:
- meson_blocks: bfloat16 [4, 8, 1024, 1024], P('tsink', 'mom')
- correlators: float32 [64, 4], P('mom', 'tsink')
The draws below stay inside these ranges and needn't reach their ends.
Inputs may be any that keep to these rules, and one draw needn't show every extreme that they name: `src_times`: distinct time slices; the first and the last time slice are always among them.
All inputs are finite; a program needn't handle non-finite values.
Results may differ from the reference program's by a relative error of at most 0.0055.
Values may be sent and summed in bfloat16 or wider, within the bound.
A program may use at most 192 MiB of HBM per device.

```python
import math
import jax
import jax.numpy as jnp
import numpy as np
from jax import lax

R = 1024
NSRC = 4
NT = 4
MOMS = 8
DIAGS = 64


def draw_src_times(key, part):
    middle = jax.random.permutation(jax.random.fold_in(key, 11), NT - 2) + 1
    picked = jnp.concatenate([jnp.array([0, NT - 1], jnp.int32), middle[:NSRC - 2].astype(jnp.int32)])
    return jax.random.permutation(jax.random.fold_in(key, 12), picked)


def plant(values, stream_key, low, top_value):
    spot = [jax.random.randint(jax.random.fold_in(stream_key, axis), (), 0, length) for axis, length in enumerate(values.shape)]
    widest = values.shape.index(max(values.shape))
    next_to = spot[:widest] + [(spot[widest] + 1) % values.shape[widest]] + spot[widest + 1:]
    return values.at[tuple(spot)].set(low).at[tuple(next_to)].set(top_value)


def steps_of(key, extent, pieces, low, largest):
    def one(position, parts):
        steps = jax.random.uniform(jax.random.fold_in(jax.random.fold_in(key, 6), position), (parts,), jnp.float32, low / len(pieces), largest / len(pieces))
        return jnp.repeat(jnp.exp(steps), extent[position] // parts).reshape((-1,) + (1,) * (len(extent) - position - 1))

    loudness = one(*pieces[0])
    for cut in pieces[1:]:
        loudness = loudness * one(*cut)
    return loudness


def rank_table(count, lean):
    portions = [(1 << 20) // math.isqrt(rank ** lean) + 1 for rank in range(1, count + 1)]
    scale = 1 + sum(portions) // (1 << 30)
    return np.cumsum(np.array([max(1, weight // scale) for weight in portions]))


def ranked(key, shape, number_of, lean):
    table = rank_table(number_of, lean)
    lot = jax.random.randint(jax.random.fold_in(key, 1), shape, 0, int(table[number_of - 1]))
    rank = jnp.searchsorted(jnp.asarray(table, jnp.int32), lot, side="right")
    return jax.random.permutation(jax.random.fold_in(key, 2), number_of)[rank].astype(jnp.int32)


def scatter_about(own_key, extent, scale, bound, pieces=(), held_as=jnp.bfloat16):
    entries = jax.random.normal(own_key, extent, jnp.float32) * scale
    if len(pieces) > 0:
        entries = steps_of(own_key, extent, pieces, -0.22, 0.18) * entries
    return jnp.clip(entries, min=-bound, max=bound).astype(held_as)


def setup_inputs(seed: int = 0) -> dict:
    keys = jax.random.split(jax.random.key(seed), 5)
    return {
        "perambulators": scatter_about(keys[0], (NT, NSRC, R, R), R ** -0.5, 0.1875, ((0, 4),)),
        "elementals": scatter_about(keys[1], (NT, MOMS, R, R), 1.0, 6.0, ((0, 4), (1, 8))),
        "src_times": draw_src_times(jax.random.fold_in(keys[4], 71), 0),
        "diagrams": plant(ranked(keys[3], (DIAGS, 2), MOMS, 2), jax.random.fold_in(keys[3], 3), 0, MOMS - 1).astype(jnp.int32),
    }


def meson_block(propagators, chosen):
    summed = jnp.zeros((R, R), jnp.float32)
    for source in range(NSRC):
        half_product = lax.dot_general(chosen[source], propagators[source], (((1,), (1,)), ((), ())), preferred_element_type=jnp.float32).astype(jnp.bfloat16)
        summed = summed + jnp.dot(propagators[source], half_product, preferred_element_type=jnp.float32)
    return summed.astype(jnp.bfloat16)


def reference(perambulators, elementals, src_times, diagrams):
    chosen_all = elementals[src_times.astype(jnp.int32)]

    def per_sink(sink):
        propagators = perambulators[sink]

        def per_momentum(moment):
            return meson_block(propagators, chosen_all[:, moment])

        return lax.map(per_momentum, jnp.arange(MOMS, dtype=jnp.int32))

    blocks_all = lax.map(per_sink, jnp.arange(NT, dtype=jnp.int32))

    def per_diagram(diagram_pair):
        first = blocks_all[:, diagram_pair[0]].astype(jnp.float32)
        second = blocks_all[:, diagram_pair[1]].astype(jnp.float32)
        return jnp.einsum("tij,tji->t", first, second) / R

    correlators = lax.map(per_diagram, diagrams)
    return blocks_all, correlators
```

```python
import functools

import jax
import jax.numpy as jnp
from jax import lax
from jax.experimental import pallas as pl
from jax.experimental.pallas import tpu as pltpu
from jax.sharding import PartitionSpec as P

LANES = 128
CHUNK = 256
BF16 = jnp.bfloat16
F32 = jnp.float32


def partner_of(index, mask, size):
    out, digit = 0, 1
    while digit < size:
        mine = lax.rem(lax.div(index, digit), 2)
        if isinstance(mask, int):
            other = (mask // digit) % 2
        else:
            other = lax.rem(lax.div(mask, digit), 2)
        out = out + digit * lax.rem(mine + other, 2)
        digit *= 2
    return out


def kernel(
    n_t, n_mom, n_src, classes, diag_count,
    src_ref, diag_ref, p_hbm, e_hbm,
    out_hbm, corr_ref,
    p, e, acc, half, meson, outbox, inbox, turned, grid, grids,
    p_sem, e_send, e_fwd, e_recv, out_sem, m_send, m_recv, g_send, g_recv,
):
    order = p.shape[1]
    n_chunk = order // CHUNK
    t = lax.axis_index("tsink")
    me = lax.axis_index("mom")

    def rows(c):
        return pl.ds(pl.multiple_of(c * CHUNK, CHUNK), CHUNK)

    p_copies = [
        pltpu.make_async_copy(p_hbm.at[s], p.at[s], p_sem.at[s]) for s in range(n_src)
    ]
    own_copies = [
        pltpu.make_async_copy(
            e_hbm.at[pl.ds(c * CHUNK, CHUNK)], e.at[0, pl.ds(c * CHUNK, CHUNK)], e_recv.at[0, c]
        )
        for c in range(n_chunk)
    ]
    for copy in p_copies + own_copies:
        copy.start()

    barrier = pltpu.get_barrier_semaphore()
    for m in range(1, n_t):
        pl.semaphore_signal(
            barrier, inc=1, device_id={"tsink": partner_of(t, m, n_t)},
            device_id_type=pl.DeviceIdType.MESH,
        )
    for m in range(1, n_mom):
        pl.semaphore_signal(
            barrier, inc=1, device_id={"mom": partner_of(me, m, n_mom)},
            device_id_type=pl.DeviceIdType.MESH,
        )
    pl.semaphore_wait(barrier, n_t - 1 + n_mom - 1)

    square = n_t == 4
    direct = (1, 2) if square else tuple(range(1, n_t))
    sends = []
    for k in range(n_chunk):
        for m in direct:
            c = (k + n_chunk // 2) % n_chunk if square and m == 2 else k
            part = pl.ds(c * CHUNK, CHUNK)
            send = pltpu.make_async_remote_copy(
                src_ref=e_hbm.at[part], dst_ref=e.at[m, part],
                send_sem=e_send.at[m, c], recv_sem=e_recv.at[m, c],
                device_id={"tsink": partner_of(t, m, n_t)},
                device_id_type=pl.DeviceIdType.MESH,
            )
            send.start()
            sends.append(send)

    def forward(slot, c):
        return pltpu.make_async_remote_copy(
            src_ref=e.at[slot, rows(c)], dst_ref=e.at[3, rows(c)],
            send_sem=e_fwd.at[c], recv_sem=e_recv.at[3, c],
            device_id={"tsink": partner_of(t, 3 - slot, n_t)},
            device_id_type=pl.DeviceIdType.MESH,
        )

    def arrived(slot, c):
        pltpu.make_async_copy(e.at[slot, rows(c)], e.at[slot, rows(c)], e_recv.at[slot, c]).wait()

    acc[...] = jnp.zeros_like(acc)
    for copy in p_copies:
        copy.wait()

    def add_chunk(slot, c):
        time = partner_of(t, slot, n_t)
        source = jnp.int32(0)
        weight = jnp.float32(0)
        for s in range(n_src):
            hit = src_ref[s] == time
            source = jnp.where(hit, jnp.int32(s), source)
            weight = jnp.where(hit, jnp.float32(1), weight)
        chunk = e[slot, rows(c), :]

        @pl.loop(0, order // CHUNK)
        def _(n):
            product = lax.dot_general(
                chunk, p[source, rows(n), :], (((1,), (1,)), ((), ())),
                preferred_element_type=F32,
            )
            if n_t > n_src:
                product = product * weight
            half[:, rows(n)] = product.astype(BF16)

        @pl.loop(0, order // CHUNK)
        def _(n):
            acc[rows(n), :] += jnp.dot(
                p[source, rows(n), rows(c)], half[...], preferred_element_type=F32
            )

    @pl.loop(0, n_chunk)
    def _(c):
        arrived(0, c)
        add_chunk(0, c)

    if square:
        @pl.loop(0, 2 * n_chunk)
        def _(k):
            later = lax.rem(k, 2)
            slot = 1 + later
            c = lax.rem(lax.div(k, 2) + later * (n_chunk // 2), n_chunk)
            arrived(slot, c)

            @pl.when(k < n_chunk)
            def _():
                forward(slot, c).start()

            add_chunk(slot, c)

        @pl.loop(0, n_chunk)
        def _(k):
            c = lax.div(k, 2) + lax.rem(k, 2) * (n_chunk // 2)
            arrived(3, c)
            add_chunk(3, c)
    else:
        @pl.loop(n_chunk, n_t * n_chunk)
        def _(k):
            slot, c = lax.div(k, n_chunk), lax.rem(k, n_chunk)
            arrived(slot, c)
            add_chunk(slot, c)

    def strip(i):
        return pl.ds(pl.multiple_of(i * LANES, LANES), LANES)

    @pl.loop(0, classes)
    def _(i):
        values = acc[strip(i), :].astype(BF16)
        meson[strip(i), :] = values
        for j in range(classes):
            outbox[lax.rem(i + j, classes), strip(i), :] = values[:, j * LANES:(j + 1) * LANES]

    def post(m):
        to = partner_of(me, m, n_mom)
        return pltpu.make_async_remote_copy(
            src_ref=outbox.at[lax.rem(to, classes)], dst_ref=inbox.at[m],
            send_sem=m_send.at[m], recv_sem=m_recv.at[m],
            device_id={"mom": to}, device_id_type=pl.DeviceIdType.MESH,
        )

    def if_class(index, action):
        if classes == n_mom:
            action()
        else:
            pl.when(index < classes)(action)

    far_first = sorted(range(1, n_mom), key=lambda m: -(m // (n_mom // 2)))
    for m in far_first:
        if_class(partner_of(me, m, n_mom), lambda: post(m).start())
    out_copy = pltpu.make_async_copy(meson, out_hbm, out_sem)
    out_copy.start()

    row = lax.broadcasted_iota(jnp.int32, grid.shape, 0)
    column = lax.broadcasted_iota(jnp.int32, grid.shape, 1)
    grid[...] = jnp.zeros_like(grid)

    def traces():
        inbox[0] = outbox[lax.rem(me, classes)]

        @pl.loop(0, n_mom)
        def _(m):
            @pl.when(m > 0)
            def _():
                pltpu.make_async_copy(inbox.at[m], inbox.at[m], m_recv.at[m]).wait()

            @pl.loop(0, classes)
            def _(i):
                j = lax.rem(me + classes - i, classes)
                turned[strip(i), :] = inbox[m, strip(j), :].astype(F32).T

            second = partner_of(me, m, n_mom)

            @pl.loop(0, m + 1)
            def _(k):
                first = partner_of(me, k, n_mom)
                value = jnp.sum(inbox[k].astype(F32) * turned[...])
                hit = ((row == first) & (column == second)) | ((row == second) & (column == first))
                grid[...] += jnp.where(hit, value, 0.0)

    if_class(me, traces)

    g_sends = []
    for m in range(1, n_mom):
        send = pltpu.make_async_remote_copy(
            src_ref=grid, dst_ref=grids.at[m],
            send_sem=g_send.at[m], recv_sem=g_recv.at[m],
            device_id={"mom": partner_of(me, m, n_mom)},
            device_id_type=pl.DeviceIdType.MESH,
        )
        send.start()
        g_sends.append(send)
    total = grid[...]
    for m, send in zip(range(1, n_mom), g_sends):
        send.wait_recv()
        total = total + grids[m]

    line = lax.broadcasted_iota(jnp.int32, (diag_count, LANES), 0)
    picked = jnp.zeros((diag_count, LANES), F32)
    for d in range(diag_count):
        first = diag_ref[me * diag_count + d, 0]
        second = diag_ref[me * diag_count + d, 1]
        value = jnp.sum(jnp.where((row == first) & (column == second), total, 0.0))
        picked = jnp.where(line == d, value, picked)
    corr_ref[...] = picked[:, :1] / order

    for send in sends + g_sends:
        send.wait_send()
    if square:
        for c in range(n_chunk):
            forward(1 if c < n_chunk // 2 else 2, c).wait_send()
    for m in far_first:
        if_class(partner_of(me, m, n_mom), lambda: post(m).wait_send())
    out_copy.wait()


def body(n_t, n_mom, perambulators, elementals, src_times, diagrams):
    n_src, order = perambulators.shape[1], perambulators.shape[2]
    classes = order // LANES
    diag_count = diagrams.shape[0] // n_mom
    n_chunk = order // CHUNK
    meson, correlators = pl.pallas_call(
        functools.partial(kernel, n_t, n_mom, n_src, classes, diag_count),
        out_shape=(
            jax.ShapeDtypeStruct((order, order), BF16),
            jax.ShapeDtypeStruct((diag_count, 1), F32),
        ),
        in_specs=[
            pl.BlockSpec(memory_space=pltpu.SMEM),
            pl.BlockSpec(memory_space=pltpu.SMEM),
            pl.BlockSpec(memory_space=pl.ANY),
            pl.BlockSpec(memory_space=pl.ANY),
        ],
        out_specs=(
            pl.BlockSpec(memory_space=pl.ANY),
            pl.BlockSpec(memory_space=pltpu.VMEM),
        ),
        scratch_shapes=[
            pltpu.VMEM((n_src, order, order), BF16),
            pltpu.VMEM((n_t, order, order), BF16),
            pltpu.VMEM((order, order), F32),
            pltpu.VMEM((CHUNK, order), BF16),
            pltpu.VMEM((order, order), BF16),
            pltpu.VMEM((classes, order, LANES), BF16),
            pltpu.VMEM((n_mom, order, LANES), BF16),
            pltpu.VMEM((order, LANES), F32),
            pltpu.VMEM((n_mom, LANES), F32),
            pltpu.VMEM((n_mom, n_mom, LANES), F32),
            pltpu.SemaphoreType.DMA((n_src,)),
            pltpu.SemaphoreType.DMA((n_t, n_chunk)),
            pltpu.SemaphoreType.DMA((n_chunk,)),
            pltpu.SemaphoreType.DMA((n_t, n_chunk)),
            pltpu.SemaphoreType.DMA,
            pltpu.SemaphoreType.DMA((n_mom,)),
            pltpu.SemaphoreType.DMA((n_mom,)),
            pltpu.SemaphoreType.DMA((n_mom,)),
            pltpu.SemaphoreType.DMA((n_mom,)),
        ],
        compiler_params=pltpu.CompilerParams(
            collective_id=0, has_side_effects=True, vmem_limit_bytes=56 * 1024 * 1024
        ),
        cost_estimate=pl.CostEstimate(
            flops=4 * n_src * order ** 3, bytes_accessed=12 * order * order * 2, transcendentals=0
        ),
    )(src_times, diagrams, perambulators[0], elementals[0, 0])
    return meson[None, None], correlators


def solution(mesh):
    in_specs = (P("tsink", None, None, None), P("tsink", "mom", None, None), P(), P())
    out_specs = (P("tsink", "mom", None, None), P("mom", "tsink"))
    run = functools.partial(body, mesh.shape["tsink"], mesh.shape["mom"])
    return jax.shard_map(run, mesh=mesh, in_specs=in_specs, out_specs=out_specs, check_vma=False)
```

```python
import functools

import jax
import jax.numpy as jnp
from jax import lax
from jax.experimental import pallas as pl
from jax.experimental.pallas import tpu as pltpu
from jax.sharding import PartitionSpec as P

LANES = 128
CHUNK = 256
UNROLL = True
EARLY = 1
BF16 = jnp.bfloat16
F32 = jnp.float32


def partner_of(index, mask, size):
    out, digit = 0, 1
    while digit < size:
        mine = lax.rem(lax.div(index, digit), 2)
        if isinstance(mask, int):
            other = (mask // digit) % 2
        else:
            other = lax.rem(lax.div(mask, digit), 2)
        out = out + digit * lax.rem(mine + other, 2)
        digit *= 2
    return out


def kernel(
    n_t, n_mom, n_src, classes, diag_count,
    src_ref, diag_ref, p_hbm, e_hbm,
    meson_ref, corr_ref,
    p, e, acc, half, outbox, inbox, turned, pairs, grid, grids,
    p_sem, e_send, e_fwd, e_recv, turn, m_send, m_recv, g_send, g_recv,
):
    order = p.shape[1]
    n_chunk = order // CHUNK
    t = lax.axis_index("tsink")
    me = lax.axis_index("mom")

    def rows(c):
        return pl.ds(pl.multiple_of(c * CHUNK, CHUNK), CHUNK)

    p_copies = [
        pltpu.make_async_copy(p_hbm.at[s], p.at[s], p_sem.at[s]) for s in range(n_src)
    ]
    own_copies = [
        pltpu.make_async_copy(
            e_hbm.at[pl.ds(c * CHUNK, CHUNK)], e.at[0, pl.ds(c * CHUNK, CHUNK)], e_recv.at[0, c]
        )
        for c in range(n_chunk)
    ]
    for copy in p_copies + own_copies:
        copy.start()

    barrier = pltpu.get_barrier_semaphore()
    for m in range(1, n_t):
        pl.semaphore_signal(
            barrier, inc=1, device_id={"tsink": partner_of(t, m, n_t)},
            device_id_type=pl.DeviceIdType.MESH,
        )
    for m in range(1, n_mom):
        pl.semaphore_signal(
            barrier, inc=1, device_id={"mom": partner_of(me, m, n_mom)},
            device_id_type=pl.DeviceIdType.MESH,
        )
    pl.semaphore_wait(barrier, n_t - 1 + n_mom - 1)

    square = n_t == 4
    direct = (1, 2) if square else tuple(range(1, n_t))
    sends = []
    for k in range(n_chunk):
        for m in direct:
            c = (k + n_chunk // 2) % n_chunk if square and m == 2 else k
            part = pl.ds(c * CHUNK, CHUNK)
            sends.append(
                pltpu.make_async_remote_copy(
                    src_ref=e_hbm.at[part], dst_ref=e.at[m, part],
                    send_sem=e_send.at[m, c], recv_sem=e_recv.at[m, c],
                    device_id={"tsink": partner_of(t, m, n_t)},
                    device_id_type=pl.DeviceIdType.MESH,
                )
            )

    def start_sends():
        for send in sends:
            send.start()

    even = lax.rem(me, 2) == 0
    pl.when(even)(start_sends)

    def forward(slot, c):
        return pltpu.make_async_remote_copy(
            src_ref=e.at[slot, rows(c)], dst_ref=e.at[3, rows(c)],
            send_sem=e_fwd.at[c], recv_sem=e_recv.at[3, c],
            device_id={"tsink": partner_of(t, 3 - slot, n_t)},
            device_id_type=pl.DeviceIdType.MESH,
        )

    def arrived(slot, c):
        pltpu.make_async_copy(e.at[slot, rows(c)], e.at[slot, rows(c)], e_recv.at[slot, c]).wait()

    acc[...] = jnp.zeros_like(acc)
    for copy in p_copies:
        copy.wait()

    def source_of(slot):
        time = partner_of(t, slot, n_t)
        source = jnp.int32(0)
        weight = jnp.float32(0)
        for s in range(n_src):
            hit = src_ref[s] == time
            source = jnp.where(hit, jnp.int32(s), source)
            weight = jnp.where(hit, jnp.float32(1), weight)
        return source, weight

    def half_chunk(slot, c, place):
        source, weight = source_of(slot)
        chunk = e[slot, rows(c), :]

        @pl.loop(0, order // CHUNK, unroll=UNROLL)
        def _(n):
            product = lax.dot_general(
                chunk, p[source, rows(n), :], (((1,), (1,)), ((), ())),
                preferred_element_type=F32,
            )
            if n_t > n_src:
                product = product * weight
            half[place, :, rows(n)] = product.astype(BF16)

    def add_chunk(slot, c):
        half_chunk(slot, c, 0)
        source, _ = source_of(slot)

        @pl.loop(0, order // CHUNK, unroll=UNROLL)
        def _(n):
            acc[rows(n), :] += jnp.dot(
                p[source, rows(n), rows(c)], half[0], preferred_element_type=F32
            )

    def step_of(k):
        slot, c = lax.div(k, n_chunk), lax.rem(k, n_chunk)
        if not square:
            return slot, c
        shift = n_chunk // 2
        near = (slot == 1) | (slot == 2)
        near_c = lax.rem(lax.div(k - n_chunk, 2) + lax.rem(k, 2) * shift, n_chunk)
        far_c = lax.div(c, 2) + lax.rem(c, 2) * shift
        slot = jnp.where(near, 1 + lax.rem(k, 2), slot)
        return slot, jnp.where(near, near_c, jnp.where(slot == 3, far_c, c))

    last = n_t * n_chunk - 2

    @pl.loop(0, last)
    def _(k):
        @pl.when((k == n_chunk) & jnp.logical_not(even))
        def _():
            pl.semaphore_wait(turn, 1)
            start_sends()

        slot, c = step_of(k)
        arrived(slot, c)
        if square:
            @pl.when((k >= n_chunk) & (k < 2 * n_chunk))
            def _():
                forward(slot, c).start()

        @pl.when((k == last - EARLY) & even)
        def _():
            pl.semaphore_signal(
                turn, inc=1, device_id={"mom": partner_of(me, 1, n_mom)},
                device_id_type=pl.DeviceIdType.MESH,
            )

        add_chunk(slot, c)

    def strip(i):
        return pl.ds(pl.multiple_of(i * LANES, LANES), LANES)

    def post(m, n):
        to = partner_of(me, m, n_mom)
        return pltpu.make_async_remote_copy(
            src_ref=outbox.at[lax.rem(to, classes), rows(n)], dst_ref=inbox.at[m, rows(n)],
            send_sem=m_send.at[m, n], recv_sem=m_recv.at[m, n],
            device_id={"mom": to}, device_id_type=pl.DeviceIdType.MESH,
        )

    def if_class(index, action):
        if classes == n_mom:
            action()
        else:
            pl.when(index < classes)(action)

    far_first = sorted(range(1, n_mom), key=lambda m: -(m // (n_mom // 2)))

    for place in range(2):
        slot, c = step_of(jnp.int32(last + place))
        arrived(slot, c)
        half_chunk(slot, c, place)
    source, _ = source_of(slot)
    columns = [rows(step_of(jnp.int32(last + place))[1]) for place in range(2)]

    @pl.loop(0, n_chunk)
    def _(n):
        values = acc[rows(n), :]
        for place in range(2):
            values = values + jnp.dot(
                p[source, rows(n), columns[place]], half[place], preferred_element_type=F32
            )
        values = values.astype(BF16)
        meson_ref[rows(n), :] = values
        for r in range(CHUNK // LANES):
            i = n * (CHUNK // LANES) + r
            for j in range(classes):
                outbox[lax.rem(i + j, classes), strip(i), :] = values[
                    r * LANES:(r + 1) * LANES, j * LANES:(j + 1) * LANES
                ]
        for m in far_first:
            if_class(partner_of(me, m, n_mom), lambda: post(m, n).start())


    row = lax.broadcasted_iota(jnp.int32, grid.shape, 0)
    column = lax.broadcasted_iota(jnp.int32, grid.shape, 1)
    pairs[...] = jnp.zeros_like(pairs)

    def traces():
        inbox[0] = outbox[lax.rem(me, classes)]

        @pl.loop(0, n_mom)
        def _(m):
            @pl.when(m > 0)
            def _():
                for n in range(n_chunk):
                    part = inbox.at[m, rows(n)]
                    pltpu.make_async_copy(part, part, m_recv.at[m, n]).wait()

            @pl.loop(0, classes, unroll=UNROLL)
            def _(i):
                j = lax.rem(me + classes - i, classes)
                turned[strip(i), :] = inbox[m, strip(j), :].astype(F32).T

            second = partner_of(me, m, n_mom)

            @pl.loop(0, m + 1)
            def _(k):
                first = partner_of(me, k, n_mom)
                pairs[second, pl.ds(first, 1), :] = jnp.sum(
                    inbox[k].astype(F32) * turned[...], axis=0, keepdims=True
                )

    if_class(me, traces)

    own = jnp.zeros_like(grid)
    for q in range(n_mom):
        own = jnp.where(column == q, jnp.sum(pairs[q], axis=1, keepdims=True), own)
    grid[...] = own

    g_sends = []
    for m in range(1, n_mom):
        send = pltpu.make_async_remote_copy(
            src_ref=grid, dst_ref=grids.at[m],
            send_sem=g_send.at[m], recv_sem=g_recv.at[m],
            device_id={"mom": partner_of(me, m, n_mom)},
            device_id_type=pl.DeviceIdType.MESH,
        )
        send.start()
        g_sends.append(send)
    total = grid[...]
    for m, send in zip(range(1, n_mom), g_sends):
        send.wait_recv()
        total = total + grids[m]

    line = lax.broadcasted_iota(jnp.int32, (diag_count, LANES), 0)
    lane = lax.broadcasted_iota(jnp.int32, (diag_count, LANES), 1)
    picked = jnp.zeros((diag_count, LANES), F32)
    for d in range(diag_count):
        first = diag_ref[0, me * diag_count + d]
        second = diag_ref[1, me * diag_count + d]
        hit = ((row == first) & (column == second)) | ((row == second) & (column == first))
        value = jnp.sum(jnp.where(hit, total, 0.0), axis=0, keepdims=True)
        picked = jnp.where(line == d, value, picked)
    picked = jnp.sum(picked, axis=1, keepdims=True) / order
    corr_ref[...] = jnp.sum(jnp.where(line == lane, picked, 0.0), axis=0, keepdims=True)[:, :diag_count]

    for send in sends + g_sends:
        send.wait_send()
    if square:
        for c in range(n_chunk):
            forward(1 if c < n_chunk // 2 else 2, c).wait_send()
    for m in far_first:
        if_class(partner_of(me, m, n_mom), lambda: pl.loop(0, n_chunk)(lambda n: post(m, n).wait_send()))


def body(n_t, n_mom, perambulators, elementals, src_times, diagrams):
    n_src, order = perambulators.shape[1], perambulators.shape[2]
    classes = order // LANES
    diag_count = diagrams.shape[0] // n_mom
    n_chunk = order // CHUNK
    meson, correlators = pl.pallas_call(
        functools.partial(kernel, n_t, n_mom, n_src, classes, diag_count),
        out_shape=(
            pltpu.VMEM((order, order), BF16),
            jax.ShapeDtypeStruct((1, diag_count), F32),
        ),
        in_specs=[
            pl.BlockSpec(memory_space=pltpu.SMEM),
            pl.BlockSpec(memory_space=pltpu.SMEM),
            pl.BlockSpec(memory_space=pl.ANY),
            pl.BlockSpec(memory_space=pl.ANY),
        ],
        out_specs=(
            pl.BlockSpec(memory_space=pltpu.VMEM),
            pl.BlockSpec(memory_space=pltpu.VMEM),
        ),
        scratch_shapes=[
            pltpu.VMEM((n_src, order, order), BF16),
            pltpu.VMEM((n_t, order, order), BF16),
            pltpu.VMEM((order, order), F32),
            pltpu.VMEM((2, CHUNK, order), BF16),
            pltpu.VMEM((classes, order, LANES), BF16),
            pltpu.VMEM((n_mom, order, LANES), BF16),
            pltpu.VMEM((order, LANES), F32),
            pltpu.VMEM((n_mom, n_mom, LANES), F32),
            pltpu.VMEM((n_mom, LANES), F32),
            pltpu.VMEM((n_mom, n_mom, LANES), F32),
            pltpu.SemaphoreType.DMA((n_src,)),
            pltpu.SemaphoreType.DMA((n_t, n_chunk)),
            pltpu.SemaphoreType.DMA((n_chunk,)),
            pltpu.SemaphoreType.DMA((n_t, n_chunk)),
            pltpu.SemaphoreType.REGULAR,
            pltpu.SemaphoreType.DMA((n_mom, n_chunk)),
            pltpu.SemaphoreType.DMA((n_mom, n_chunk)),
            pltpu.SemaphoreType.DMA((n_mom,)),
            pltpu.SemaphoreType.DMA((n_mom,)),
        ],
        compiler_params=pltpu.CompilerParams(
            collective_id=0, has_side_effects=True, vmem_limit_bytes=50 * 1024 * 1024
        ),
        cost_estimate=pl.CostEstimate(
            flops=4 * n_src * order ** 3, bytes_accessed=12 * order * order * 2, transcendentals=0
        ),
    )(src_times, diagrams.T, perambulators[0], elementals[0, 0])
    return meson[None, None], correlators.T


def solution(mesh):
    in_specs = (P("tsink", None, None, None), P("tsink", "mom", None, None), P(), P())
    out_specs = (P("tsink", "mom", None, None), P("mom", "tsink"))
    run = functools.partial(body, mesh.shape["tsink"], mesh.shape["mom"])
    return jax.shard_map(run, mesh=mesh, in_specs=in_specs, out_specs=out_specs, check_vma=False)
```

```python
import functools

import jax
import jax.numpy as jnp
from jax import lax
from jax.experimental import pallas as pl
from jax.experimental.pallas import tpu as pltpu
from jax.sharding import PartitionSpec as P

LANES = 128
CHUNK = 256
UNROLL = True
EARLY = 1
BF16 = jnp.bfloat16
F32 = jnp.float32


def partner_of(index, mask, size):
    out, digit = 0, 1
    while digit < size:
        mine = lax.rem(lax.div(index, digit), 2)
        if isinstance(mask, int):
            other = (mask // digit) % 2
        else:
            other = lax.rem(lax.div(mask, digit), 2)
        out = out + digit * lax.rem(mine + other, 2)
        digit *= 2
    return out


def kernel(
    n_t, n_mom, n_src, classes, diag_count,
    src_ref, diag_ref, p_hbm, e_hbm,
    meson_ref, corr_ref,
    p, e, acc, half, outbox, inbox, turned, pairs, grid, grids,
    p_sem, e_send, e_fwd, e_recv, turn, m_send, m_recv, g_send, g_recv,
):
    order = p.shape[1]
    n_chunk = order // CHUNK
    t = lax.axis_index("tsink")
    me = lax.axis_index("mom")

    def rows(c):
        return pl.ds(pl.multiple_of(c * CHUNK, CHUNK), CHUNK)

    p_copies = [
        pltpu.make_async_copy(p_hbm.at[s], p.at[s], p_sem.at[s]) for s in range(n_src)
    ]
    own_copies = [
        pltpu.make_async_copy(
            e_hbm.at[pl.ds(c * CHUNK, CHUNK)], e.at[0, pl.ds(c * CHUNK, CHUNK)], e_recv.at[0, c]
        )
        for c in range(n_chunk)
    ]
    for copy in p_copies + own_copies:
        copy.start()

    barrier = pltpu.get_barrier_semaphore()
    for m in range(1, n_t):
        pl.semaphore_signal(
            barrier, inc=1, device_id={"tsink": partner_of(t, m, n_t)},
            device_id_type=pl.DeviceIdType.MESH,
        )
    for m in range(1, n_mom):
        pl.semaphore_signal(
            barrier, inc=1, device_id={"mom": partner_of(me, m, n_mom)},
            device_id_type=pl.DeviceIdType.MESH,
        )
    pl.semaphore_wait(barrier, n_t - 1 + n_mom - 1)

    square = n_t == 4
    direct = (1, 2) if square else tuple(range(1, n_t))
    sends = []
    for k in range(n_chunk):
        for m in direct:
            c = (k + n_chunk // 2) % n_chunk if square and m == 2 else k
            part = pl.ds(c * CHUNK, CHUNK)
            sends.append(
                pltpu.make_async_remote_copy(
                    src_ref=e_hbm.at[part], dst_ref=e.at[m, part],
                    send_sem=e_send.at[m, c], recv_sem=e_recv.at[m, c],
                    device_id={"tsink": partner_of(t, m, n_t)},
                    device_id_type=pl.DeviceIdType.MESH,
                )
            )

    def start_sends():
        for send in sends:
            send.start()

    even = lax.rem(me, 2) == 0
    pl.when(even)(start_sends)

    def forward(slot, c):
        return pltpu.make_async_remote_copy(
            src_ref=e.at[slot, rows(c)], dst_ref=e.at[3, rows(c)],
            send_sem=e_fwd.at[c], recv_sem=e_recv.at[3, c],
            device_id={"tsink": partner_of(t, 3 - slot, n_t)},
            device_id_type=pl.DeviceIdType.MESH,
        )

    def arrived(slot, c):
        pltpu.make_async_copy(e.at[slot, rows(c)], e.at[slot, rows(c)], e_recv.at[slot, c]).wait()

    acc[...] = jnp.zeros_like(acc)
    for copy in p_copies:
        copy.wait()

    def source_of(slot):
        time = partner_of(t, slot, n_t)
        source = jnp.int32(0)
        weight = jnp.float32(0)
        for s in range(n_src):
            hit = src_ref[s] == time
            source = jnp.where(hit, jnp.int32(s), source)
            weight = jnp.where(hit, jnp.float32(1), weight)
        return source, weight

    def half_chunk(slot, c, place):
        source, weight = source_of(slot)
        chunk = e[slot, rows(c), :]

        @pl.loop(0, order // CHUNK, unroll=UNROLL)
        def _(n):
            product = lax.dot_general(
                chunk, p[source, rows(n), :], (((1,), (1,)), ((), ())),
                preferred_element_type=F32,
            )
            if n_t > n_src:
                product = product * weight
            half[place, :, rows(n)] = product.astype(BF16)

    def add_chunk(slot, c):
        half_chunk(slot, c, 0)
        source, _ = source_of(slot)

        @pl.loop(0, order // CHUNK, unroll=UNROLL)
        def _(n):
            acc[rows(n), :] += jnp.dot(
                p[source, rows(n), rows(c)], half[0], preferred_element_type=F32
            )

    def step_of(k):
        slot, c = lax.div(k, n_chunk), lax.rem(k, n_chunk)
        if not square:
            return slot, c
        shift = n_chunk // 2
        near = (slot == 1) | (slot == 2)
        near_c = lax.rem(lax.div(k - n_chunk, 2) + lax.rem(k, 2) * shift, n_chunk)
        far_c = lax.div(c, 2) + lax.rem(c, 2) * shift
        slot = jnp.where(near, 1 + lax.rem(k, 2), slot)
        return slot, jnp.where(near, near_c, jnp.where(slot == 3, far_c, c))

    last = n_t * n_chunk - 2

    @pl.loop(0, last)
    def _(k):
        @pl.when((k == n_chunk) & jnp.logical_not(even))
        def _():
            pl.semaphore_wait(turn, 1)
            start_sends()

        slot, c = step_of(k)
        arrived(slot, c)
        if square:
            @pl.when((k >= n_chunk) & (k < 2 * n_chunk))
            def _():
                forward(slot, c).start()

        @pl.when((k == last - EARLY) & even)
        def _():
            pl.semaphore_signal(
                turn, inc=1, device_id={"mom": partner_of(me, 1, n_mom)},
                device_id_type=pl.DeviceIdType.MESH,
            )

        add_chunk(slot, c)

    def strip(i):
        return pl.ds(pl.multiple_of(i * LANES, LANES), LANES)

    def post(m, n):
        to = partner_of(me, m, n_mom)
        return pltpu.make_async_remote_copy(
            src_ref=outbox.at[lax.rem(to, classes), rows(n)], dst_ref=inbox.at[m, rows(n)],
            send_sem=m_send.at[m, n], recv_sem=m_recv.at[m, n],
            device_id={"mom": to}, device_id_type=pl.DeviceIdType.MESH,
        )

    def if_class(index, action):
        if classes == n_mom:
            action()
        else:
            pl.when(index < classes)(action)

    far_first = sorted(range(1, n_mom), key=lambda m: -(m // (n_mom // 2)))

    for place in range(2):
        slot, c = step_of(jnp.int32(last + place))
        arrived(slot, c)
        half_chunk(slot, c, place)
    source, _ = source_of(slot)
    columns = [rows(step_of(jnp.int32(last + place))[1]) for place in range(2)]

    @pl.loop(0, n_chunk)
    def _(n):
        values = acc[rows(n), :]
        for place in range(2):
            values = values + jnp.dot(
                p[source, rows(n), columns[place]], half[place], preferred_element_type=F32
            )
        values = values.astype(BF16)
        meson_ref[rows(n), :] = values
        for r in range(CHUNK // LANES):
            i = n * (CHUNK // LANES) + r
            for j in range(classes):
                outbox[lax.rem(i + j, classes), strip(i), :] = values[
                    r * LANES:(r + 1) * LANES, j * LANES:(j + 1) * LANES
                ]
        for m in far_first:
            if_class(partner_of(me, m, n_mom), lambda: post(m, n).start())


    row = lax.broadcasted_iota(jnp.int32, grid.shape, 0)
    column = lax.broadcasted_iota(jnp.int32, grid.shape, 1)
    pairs[...] = jnp.zeros_like(pairs)

    def traces():
        inbox[0] = outbox[lax.rem(me, classes)]

        def in_order(position):
            group = lax.div(position, n_mom // 2) + lax.rem(me, 2)
            return 2 * lax.rem(position, n_mom // 2) + lax.rem(group, 2)

        @pl.loop(0, n_mom)
        def _(position):
            m = in_order(position)

            @pl.when(m > 0)
            def _():
                for n in range(n_chunk):
                    part = inbox.at[m, rows(n)]
                    pltpu.make_async_copy(part, part, m_recv.at[m, n]).wait()

            @pl.loop(0, classes, unroll=UNROLL)
            def _(i):
                j = lax.rem(me + classes - i, classes)
                turned[strip(i), :] = inbox[m, strip(j), :].astype(F32).T

            second = partner_of(me, m, n_mom)

            @pl.loop(0, position + 1)
            def _(earlier):
                k = in_order(earlier)
                first = partner_of(me, k, n_mom)
                pairs[second, pl.ds(first, 1), :] = jnp.sum(
                    inbox[k].astype(F32) * turned[...], axis=0, keepdims=True
                )

    if_class(me, traces)

    own = jnp.zeros_like(grid)
    for q in range(n_mom):
        own = jnp.where(column == q, jnp.sum(pairs[q], axis=1, keepdims=True), own)
    grid[...] = own

    g_sends = []
    for m in range(1, n_mom):
        send = pltpu.make_async_remote_copy(
            src_ref=grid, dst_ref=grids.at[m],
            send_sem=g_send.at[m], recv_sem=g_recv.at[m],
            device_id={"mom": partner_of(me, m, n_mom)},
            device_id_type=pl.DeviceIdType.MESH,
        )
        send.start()
        g_sends.append(send)
    total = grid[...]
    for m, send in zip(range(1, n_mom), g_sends):
        send.wait_recv()
        total = total + grids[m]

    line = lax.broadcasted_iota(jnp.int32, (diag_count, LANES), 0)
    lane = lax.broadcasted_iota(jnp.int32, (diag_count, LANES), 1)
    picked = jnp.zeros((diag_count, LANES), F32)
    for d in range(diag_count):
        first = diag_ref[0, me * diag_count + d]
        second = diag_ref[1, me * diag_count + d]
        hit = ((row == first) & (column == second)) | ((row == second) & (column == first))
        value = jnp.sum(jnp.where(hit, total, 0.0), axis=0, keepdims=True)
        picked = jnp.where(line == d, value, picked)
    picked = jnp.sum(picked, axis=1, keepdims=True) / order
    corr_ref[...] = jnp.sum(jnp.where(line == lane, picked, 0.0), axis=0, keepdims=True)[:, :diag_count]

    for send in sends + g_sends:
        send.wait_send()
    if square:
        for c in range(n_chunk):
            forward(1 if c < n_chunk // 2 else 2, c).wait_send()
    for m in far_first:
        if_class(partner_of(me, m, n_mom), lambda: pl.loop(0, n_chunk)(lambda n: post(m, n).wait_send()))


def body(n_t, n_mom, perambulators, elementals, src_times, diagrams):
    n_src, order = perambulators.shape[1], perambulators.shape[2]
    classes = order // LANES
    diag_count = diagrams.shape[0] // n_mom
    n_chunk = order // CHUNK
    meson, correlators = pl.pallas_call(
        functools.partial(kernel, n_t, n_mom, n_src, classes, diag_count),
        out_shape=(
            pltpu.VMEM((order, order), BF16),
            jax.ShapeDtypeStruct((1, diag_count), F32),
        ),
        in_specs=[
            pl.BlockSpec(memory_space=pltpu.SMEM),
            pl.BlockSpec(memory_space=pltpu.SMEM),
            pl.BlockSpec(memory_space=pl.ANY),
            pl.BlockSpec(memory_space=pl.ANY),
        ],
        out_specs=(
            pl.BlockSpec(memory_space=pltpu.VMEM),
            pl.BlockSpec(memory_space=pltpu.VMEM),
        ),
        scratch_shapes=[
            pltpu.VMEM((n_src, order, order), BF16),
            pltpu.VMEM((n_t, order, order), BF16),
            pltpu.VMEM((order, order), F32),
            pltpu.VMEM((2, CHUNK, order), BF16),
            pltpu.VMEM((classes, order, LANES), BF16),
            pltpu.VMEM((n_mom, order, LANES), BF16),
            pltpu.VMEM((order, LANES), F32),
            pltpu.VMEM((n_mom, n_mom, LANES), F32),
            pltpu.VMEM((n_mom, LANES), F32),
            pltpu.VMEM((n_mom, n_mom, LANES), F32),
            pltpu.SemaphoreType.DMA((n_src,)),
            pltpu.SemaphoreType.DMA((n_t, n_chunk)),
            pltpu.SemaphoreType.DMA((n_chunk,)),
            pltpu.SemaphoreType.DMA((n_t, n_chunk)),
            pltpu.SemaphoreType.REGULAR,
            pltpu.SemaphoreType.DMA((n_mom, n_chunk)),
            pltpu.SemaphoreType.DMA((n_mom, n_chunk)),
            pltpu.SemaphoreType.DMA((n_mom,)),
            pltpu.SemaphoreType.DMA((n_mom,)),
        ],
        compiler_params=pltpu.CompilerParams(
            collective_id=0, has_side_effects=True, vmem_limit_bytes=50 * 1024 * 1024
        ),
        cost_estimate=pl.CostEstimate(
            flops=4 * n_src * order ** 3, bytes_accessed=12 * order * order * 2, transcendentals=0
        ),
    )(src_times, diagrams.T, perambulators[0], elementals[0, 0])
    return meson[None, None], correlators.T


def solution(mesh):
    in_specs = (P("tsink", None, None, None), P("tsink", "mom", None, None), P(), P())
    out_specs = (P("tsink", "mom", None, None), P("mom", "tsink"))
    run = functools.partial(body, mesh.shape["tsink"], mesh.shape["mom"])
    return jax.shard_map(run, mesh=mesh, in_specs=in_specs, out_specs=out_specs, check_vma=False)
```
